32 devices in a mesh: dp: 4 (over y, x), tensor: 2 (over core), seq: 4 (over z).
Axes of the slice: x: 2, y: 2, z: 4, core: 2. Of those that a mesh axis runs over, the one named last changes fastest.
Arguments:
- tokens: bfloat16 [8, 1024, 1472], P(('dp', 'tensor'), 'seq'), may hold values from -6 to 6
- segment_ids: int32 [8, 1024], P('dp'), may hold values from 0 to 7, never falling along the last dimension, each value on 1 to 896 neighbouring positions
- buckets: int32 [2047], replicated, may hold values from 0 to 31, as said below
- gain_attn: bfloat16 [1472], replicated, may hold values from 0.5 to 1.5
- w_query: bfloat16 [1472, 384], P(None, 'tensor'), may hold values from -0.078125 to 0.078125
- w_key: bfloat16 [1472, 384], P(None, 'tensor'), may hold values from -0.078125 to 0.078125
- w_value: bfloat16 [1472, 384], P(None, 'tensor'), may hold values from -0.15625 to 0.15625
- w_out: bfloat16 [1472, 384], P(None, 'tensor'), may hold values from -1.25 to 1.25
- rel_table: bfloat16 [32, 6], P(None, 'tensor'), may hold values from -4 to 4
- gain_ff: bfloat16 [1472], replicated, may hold values from 0.5 to 1.5
- w_gate: bfloat16 [1472, 3584], P(None, 'tensor'), may hold values from -0.15625 to 0.15625
- w_up: bfloat16 [1472, 3584], P(None, 'tensor'), may hold values from -0.15625 to 0.15625
- w_down: bfloat16 [1472, 3584], P(None, 'tensor'), may hold values from -0.125 to 0.125
- cotangent: bfloat16 [8, 1024, 1472], P(('dp', 'tensor'), 'seq'), may hold values from -6 to 6
Outputs:
- layer_out: float32 [8, 1024, 1472], P(('dp', 'tensor'), 'seq')
- grad_tokens: float32 [8, 1024, 1472], P(('dp', 'tensor'), 'seq')
- grad_gain_attn: float32 [1472], replicated
- grad_w_query: float32 [1472, 384], P('dp', ('tensor', 'seq'))
- grad_w_key: float32 [1472, 384], P('dp', ('tensor', 'seq'))
- grad_w_value: float32 [1472, 384], P('dp', ('tensor', 'seq'))
- grad_w_out: float32 [1472, 384], P('dp', ('tensor', 'seq'))
- grad_rel_table: float32 [32, 6], replicated
- grad_gain_ff: float32 [1472], replicated
- grad_w_gate: float32 [1472, 3584], P('dp', ('tensor', 'seq'))
- grad_w_up: float32 [1472, 3584], P('dp', ('tensor', 'seq'))
- grad_w_down: float32 [1472, 3584], P('dp', ('tensor', 'seq'))
The draws below stay inside these ranges and needn't reach their ends.
Inputs may be any that keep to these rules, and one draw needn't show every extreme that they name: `segment_ids`: within a row the ids never fall; a document holds 1 to 896 positions, and in every row one holds exactly 896. `buckets`: the bucket depends only on the offset d: it is 0 at d = 0, never falls as |d| grows with d's sign fixed, and is raised by 16 for d > 0.
All inputs are finite; a program needn't handle non-finite values.
Results may differ from the reference program's by a relative error of at most 0.022.
Values may be sent and summed in bfloat16 or wider, within the bound.
A program may use at most 192 MiB of HBM per device.

```python
import math
import jax
import jax.numpy as jnp
import numpy as np
from jax import lax

D = 1472
H = 6
DH = 64
FF = 3584
NB = 32
L = 1024
INNER = 384
ROWS = 8


def draw_buckets(key, part):
    half_count = NB // 2
    steps_all = jax.random.randint(key, (half_count - 1,), 1, max(3, L // NB), dtype=jnp.int32)
    bounds = jnp.cumsum(steps_all).astype(jnp.int32)
    offsets = jnp.arange(2 * L - 1, dtype=jnp.int32) - (L - 1)
    levels = jnp.sum((jnp.abs(offsets)[:, None] >= bounds[None, :]).astype(jnp.int32), axis=1)
    return levels + half_count * (offsets > 0).astype(jnp.int32)


def raised(entries, rng, source, target, parts, factor):
    def block_of(position):
        return (jnp.arange(entries.shape[position]) // (entries.shape[position] // parts)).reshape((-1,) + (1,) * (entries.ndim - 1 - position))

    near = jax.random.permutation(rng, parts)[block_of(target)]
    other_side = (block_of(target) + parts // 2) % parts
    return jnp.where((block_of(source) == near) | (block_of(source) == other_side), factor * entries, entries)


def shard_levels(stream_key, shape, cuts, low, high):
    level, own = 1.0, jax.random.fold_in(stream_key, 6)
    for position, shards_of in cuts:
        draws = jnp.exp(jax.random.uniform(jax.random.fold_in(own, position), (shards_of,), jnp.float32, low / len(cuts), high / len(cuts)))
        level = level * jnp.repeat(draws, shape[position] // shards_of).reshape([-1 if axis == position else 1 for axis in range(len(shape))])
    return level


def split_up(count, total, most, lean):
    weights = [(1 << 20) // math.isqrt(grade ** lean) + 1 for grade in range(2, count + 1)]
    spare, given = total - most - (count - 1), [1] * (count - 1)
    while spare > 0:
        free = [i for i in range(count - 1) if given[i] < most]
        mass, budget = sum([weights[i] for i in free]), spare
        for i in free:
            addition = min(most - given[i], max(1, budget * weights[i] // mass), spare)
            given[i] = given[i] + addition
            spare = spare - addition
    return np.array([most] + given)


def ragged(stream_key, amount, total, bound, lean):
    if amount == 2:
        one = jax.random.randint(stream_key, (), max(1, total - bound), min(bound, total - 1) + 1)
        return jnp.stack([one, total - one])
    lengths = jnp.asarray(split_up(amount, total, bound, lean), jnp.int32)
    pairs = (amount - 1) // 2
    donor, taker = lengths[1:1 + 2 * pairs:2], lengths[2:2 + 2 * pairs:2]
    room = jnp.minimum(donor - 1, bound - taker)
    shifted = jax.random.randint(jax.random.fold_in(stream_key, 1), (pairs,), 0, 1 << 20) % (room + 1)
    lengths = lengths.at[1:1 + 2 * pairs:2].set(donor - shifted).at[2:2 + 2 * pairs:2].set(taker + shifted)
    return lengths[jax.random.permutation(jax.random.fold_in(stream_key, 2), amount)]


def normal_values(stream_key, extent, width, reach, cuts=(), held_as=jnp.bfloat16):
    loudness = shard_levels(stream_key, extent, cuts, -0.22, 0.18) if cuts else 1.0
    array = jax.random.normal(stream_key, extent, jnp.float32) * width * loudness
    return jnp.minimum(jnp.maximum(array, -reach), reach).astype(held_as)


def heavy_noise(stream_key, shape, spread, reach, shards, heavy, kind=jnp.bfloat16):
    drawn = spread * jax.random.normal(stream_key, shape, jnp.float32)
    if shards:
        drawn = drawn * shard_levels(stream_key, shape, shards, -0.22, 0.18)
    return jnp.clip(raised(drawn, jax.random.fold_in(stream_key, 3), *heavy), -reach, reach).astype(kind)


def setup_inputs(seed: int = 0) -> dict:
    key_list = jax.random.split(jax.random.key(seed), 15)
    return {
        "tokens": heavy_noise(key_list[0], (ROWS, L, D), 1.0, 6.0, ((0, 8), (1, 4)), (0, 2, 8, 2.0)),
        "segment_ids": jax.vmap(lambda own: jnp.searchsorted(jnp.cumsum(ragged(own, max(3, L // 128), L, L - L // 8, 1)), jnp.arange(L), side="right"))(jax.random.split(key_list[1], ROWS)).reshape((ROWS, L)).astype(jnp.int32),
        "buckets": draw_buckets(jax.random.fold_in(key_list[14], 71), 0),
        "gain_attn": jnp.clip(1.0 + 0.1 * jax.random.normal(key_list[3], (D,), jnp.float32), 0.5, 1.5).astype(jnp.bfloat16),
        "w_query": normal_values(key_list[4], (D, INNER), (4 * D) ** -0.5, 0.078125, ((1, 2),)),
        "w_key": normal_values(key_list[5], (D, INNER), (4 * D) ** -0.5, 0.078125, ((1, 2),)),
        "w_value": normal_values(key_list[6], (D, INNER), D ** -0.5, 0.15625, ((1, 2),)),
        "w_out": normal_values(key_list[7], (D, INNER), (INNER // 16) ** -0.5, 1.25, ((1, 2),)),
        "rel_table": normal_values(key_list[8], (NB, H), 1.0, 4.0, ((1, 2),)),
        "gain_ff": jnp.clip(1.0 + 0.1 * jax.random.normal(key_list[9], (D,), jnp.float32), 0.5, 1.5).astype(jnp.bfloat16),
        "w_gate": normal_values(key_list[10], (D, FF), D ** -0.5, 0.15625, ((1, 2),)),
        "w_up": normal_values(key_list[11], (D, FF), D ** -0.5, 0.15625, ((1, 2),)),
        "w_down": normal_values(key_list[12], (D, FF), (FF // 2) ** -0.5, 0.125, ((1, 2),)),
        "cotangent": heavy_noise(key_list[13], (ROWS, L, D), 1.0, 6.0, ((0, 8), (1, 4)), (0, 2, 8, 2.0)),
    }


@jax.custom_vjp
def low(v):
    return lax.optimization_barrier(v.astype(jnp.bfloat16)).astype(jnp.float32)

@jax.custom_vjp
def low_back(v):
    return v

def low_keep(v):
    return (low(v), None)

def low_pass(kept, grad):
    return (grad,)

def back_keep(v):
    return (v, None)

def back_low(kept, grad):
    return (low(grad),)
low.defvjp(low_keep, low_pass)
low_back.defvjp(back_keep, back_low)
highest = lax.Precision.HIGHEST
gelu_scale = math.sqrt(2.0 / math.pi)

def gelu_tanh(values):
    return 0.5 * values * (1.0 + jnp.tanh(gelu_scale * (values + 0.044715 * values * values * values)))

def rms_scale(values, gain_vec):
    return values * lax.rsqrt(lax.optimization_barrier(jnp.mean(values * values, axis=-1, keepdims=True)) + 1e-06) * gain_vec

def attn_block(queries, keys, values, segments, pos_bias):
    raw_scores = low_back(jnp.einsum('rqhd,rkhd->rhqk', queries, keys, precision=highest) + pos_bias[None])
    same_doc = segments[:, None, :, None] == segments[:, None, None, :]
    scores = jnp.where(same_doc, raw_scores, -1e+30)
    row_max = lax.optimization_barrier(jnp.max(scores, axis=-1, keepdims=True))
    exp_scores = jnp.exp(scores - row_max)
    attn_probs = low(exp_scores / lax.optimization_barrier(jnp.sum(exp_scores, axis=-1, keepdims=True)))
    return jnp.einsum('rhqk,rkhd->rqhd', attn_probs, values, precision=highest)

def reference(tokens, segment_ids, buckets, gain_attn, w_query, w_key, w_value, w_out, rel_table, gain_ff, w_gate, w_up, w_down, cotangent):
    positions = jnp.arange(L, dtype=jnp.int32)
    offset_index = positions[None, :] - positions[:, None] + (L - 1)
    group_count = ROWS // 4
    seg_groups = segment_ids.reshape(group_count, 4, L)

    def project(normed, weight):
        return jnp.einsum('rld,de->rle', normed, weight, precision=highest)

    def head_groups(values):
        return values.reshape(group_count, 4, L, H, DH)

    def whole_layer(tokens_f, gain_one, query_mat, key_mat, value_mat, out_mat, table_mat, gain_two, gate_mat, up_mat, down_mat):
        normed = low(rms_scale(tokens_f, gain_one))
        queries = low_back(low(project(normed, query_mat)))
        keys = low_back(low(project(normed, key_mat)))
        values = low_back(low(project(normed, value_mat)))
        per_offset = table_mat[buckets]
        pos_bias = jnp.transpose(per_offset[offset_index], (2, 0, 1))

        def scan_step(loop_state, pieces):
            return (loop_state, jax.checkpoint(attn_block)(pieces[0], pieces[1], pieces[2], pieces[3], pos_bias))
        loop_state, context = lax.scan(scan_step, jnp.zeros((), jnp.float32), (head_groups(queries), head_groups(keys), head_groups(values), seg_groups))
        context = low_back(low(context.reshape(ROWS, L, H * DH)))
        attn_branch = low_back(jnp.einsum('rle,de->rld', context, out_mat, precision=highest))
        after_attn = tokens_f + attn_branch
        normed_ff = low(rms_scale(after_attn, gain_two))
        gate_pre = low_back(project(normed_ff, gate_mat))
        up_pre = low_back(project(normed_ff, up_mat))
        hidden = low(gelu_tanh(gate_pre) * up_pre)
        ff_branch = low_back(jnp.einsum('rlf,df->rld', hidden, down_mat, precision=highest))
        return after_attn + ff_branch
    layer_out, pull_back = jax.vjp(whole_layer, tokens.astype(jnp.float32), gain_attn.astype(jnp.float32), w_query.astype(jnp.float32), w_key.astype(jnp.float32), w_value.astype(jnp.float32), w_out.astype(jnp.float32), rel_table.astype(jnp.float32), gain_ff.astype(jnp.float32), w_gate.astype(jnp.float32), w_up.astype(jnp.float32), w_down.astype(jnp.float32))
    grads = pull_back(cotangent.astype(jnp.float32))
    return (layer_out, grads[0], grads[1], grads[2], grads[3], grads[4], grads[5], grads[6], grads[7], grads[8], grads[9], grads[10])
```

```python
import math

import jax
import jax.numpy as jnp
from jax import lax
from jax.experimental import pallas as pl
from jax.experimental.pallas import tpu as pltpu
from jax.sharding import PartitionSpec as P

eps_norm = 1e-06
gelu_scale = math.sqrt(2.0 / math.pi)
masked_score = -1e30
highest = lax.Precision.HIGHEST


def shortened(shard):

    def short(part):
        return part.astype(jnp.bfloat16) if part.dtype == jnp.float32 else part

    return jax.tree.map(short, shard)


def gelu_tanh(values):
    return (
        0.5 * values * (1.0 + jnp.tanh(gelu_scale * (values + 0.044715 * values * values * values)))
    )


def rms_scale(values, gain_vec):
    return (
        values * lax.rsqrt(jnp.mean(values * values, axis=-1, keepdims=True) + eps_norm) * gain_vec
    )


def gated_unit(gate_pre, up_pre):
    return gelu_tanh(gate_pre) * up_pre


def token_sum(left, right):
    left_flat = left.reshape(-1, left.shape[-1])
    right_flat = right.reshape(-1, right.shape[-1])
    return lax.dot_general(
        left_flat, right_flat, (((0,), (0,)), ((), ())), preferred_element_type=jnp.float32
    )


def times_weight_t(values, weight):
    return lax.dot_general(
        values, weight, (((values.ndim - 1,), (1,)), ((), ())), preferred_element_type=jnp.float32
    )


def toeplitz_rows(window, row_count, col_count):
    window_len = window.shape[1]
    turned = jnp.roll(window, -(row_count - 1), axis=1)
    repeated = jnp.tile(turned, (1, row_count))[:, : row_count * (window_len - 1)]
    return repeated.reshape(window.shape[0], row_count, window_len - 1)[:, :, :col_count]


def diagonal_sums(score_block):
    head_count, row_count, col_count = score_block.shape
    flipped = jnp.flip(score_block, axis=1)
    padded = jnp.pad(flipped, ((0, 0), (0, 0), (0, row_count)))
    sheared = padded.reshape(head_count, row_count * (col_count + row_count))
    sheared = sheared[:, : row_count * (col_count + row_count - 1)]
    return jnp.sum(sheared.reshape(head_count, row_count, col_count + row_count - 1), axis=1)


f32, bf16 = jnp.float32, jnp.bfloat16
MESH = pl.DeviceIdType.MESH
NT = (((1,), (1,)), ((), ()))
TN = (((0,), (0,)), ((), ()))


def dot_f32(left, right, dims=(((1,), (0,)), ((), ()))):
    return lax.dot_general(left, right, dims, preferred_element_type=f32)


class Links:
    def __init__(self, send_sems, recv_sems):
        self.send_sems, self.recv_sems, self.count, self.open = send_sems, recv_sems, 0, []
        dp, core, seq = lax.axis_index("dp"), lax.axis_index("tensor"), lax.axis_index("seq")
        self.dp, self.t, self.s = dp, core, seq
        self.x = lax.rem(dp, 2)
        self.y = lax.div(dp, 2)
        self.core = (dp, 1 - core, seq)
        self.xdev = (dp + 1 - 2 * self.x, core, seq)
        self.ydev = (dp + 2 - 4 * self.y, core, seq)

    def z(self, step):
        return (self.dp, self.t, lax.rem(self.s + step + 4, 4))

    def to_seq(self, target):
        return (self.dp, self.t, target)

    def slots(self, amount=1):
        first = self.count
        self.count += amount
        return first

    def copy(self, src, dst, device, slot=None):
        slot = self.slots() if slot is None else slot
        return pltpu.make_async_remote_copy(
            src_ref=src,
            dst_ref=dst,
            send_sem=self.send_sems.at[slot],
            recv_sem=self.recv_sems.at[slot],
            device_id=device,
            device_id_type=MESH,
        )

    def send(self, src, dst, device):
        single = self.copy(src, dst, device)
        single.start()
        self.open.append(single)
        return single

    def finish(self):
        for single in self.open:
            single.wait_send()
        self.open = []

    def greet(self, devices):
        barrier = pltpu.get_barrier_semaphore()
        for device in devices:
            pl.semaphore_signal(barrier, inc=1, device_id=device, device_id_type=MESH)
        pl.semaphore_wait(barrier, len(devices))


def unit_scale(values):
    return lax.rsqrt(jnp.mean(values * values, axis=-1, keepdims=True) + eps_norm)


def forward_kernel(
    tokens,
    cotangent,
    seg_rows,
    bucket_window,
    table_t,
    gain_attn,
    gain_ff,
    w_query,
    w_key,
    w_value,
    w_out,
    normed_pair,
    queries,
    pairs,
    context,
    log_total,
    after_attn,
    ff_pair,
    cot_pair,
    cot_near,
    bias,
    per_offset,
    send_buf,
    recv_buf,
    local_sem,
    send_sems,
    recv_sems,
):
    links = Links(send_sems, recv_sems)
    t, s = links.t, links.s
    rows, pos, width = normed_pair.shape
    inner = queries.shape[2]
    heads = bias.shape[0]
    dh = inner // heads
    links.greet([links.core, links.xdev, links.z(1), links.z(2), links.z(3)])
    own_cot = pltpu.make_async_copy(cotangent, cot_pair.at[t], local_sem)
    own_cot.start()
    cot_core = links.send(cotangent, cot_pair.at[t], links.core)
    cot_x = links.send(cotangent, cot_near.at[t], links.xdev)

    values = tokens[...].astype(f32)
    normed_pair[t] = (values * unit_scale(values) * gain_attn[...]).astype(bf16)
    normed_core = links.send(normed_pair.at[t], normed_pair.at[t], links.core)

    chain = links.slots(2 * 3 * 2)

    def hop(way, step, row):
        slot = chain + (way * 3 + step - 1) * 2 + row
        step_by = 1 if way == 0 else -1
        block = lax.rem(s - step_by * (step - 1) + 4, 4)
        place = lax.rem(t + row, 2)
        return links.copy(
            pairs.at[block, place], pairs.at[block, place], links.z(step_by), slot
        )

    def sends(way, step):
        return (s >= step - 1) & (s < 3) if way == 0 else (s <= 4 - step) & (s > 0)

    def receives(way, step):
        return s >= step if way == 0 else s <= 3 - step

    def project(place, row):
        block = normed_pair[place]
        queries[place] = dot_f32(block, w_query[...]).astype(bf16)
        pairs[s, place] = jnp.concatenate(
            [dot_f32(block, w_key[...]), dot_f32(block, w_value[...])], axis=1
        ).astype(bf16)
        for way in range(2):
            pl.when(sends(way, 1))(lambda way=way: hop(way, 1, row).start())

    project(t, 0)
    normed_core.wait_recv()
    project(1 - t, 1)

    bucket_ids = lax.broadcasted_iota(jnp.int32, (table_t.shape[1], bucket_window.shape[1]), 0)
    one_hot = (bucket_ids == bucket_window[...]).astype(bf16)
    per_offset[...] = dot_f32(table_t[...], one_hot)
    window = per_offset[:, pl.ds(pl.multiple_of(s * pos, 128), 5 * pos)]
    for head in range(heads):
        for block in range(4):
            strip = jnp.concatenate(
                [
                    window[head : head + 1, (4 - block) * pos : (5 - block) * pos],
                    window[head : head + 1, (3 - block) * pos : (4 - block) * pos],
                ],
                axis=1,
            )
            strip = jnp.broadcast_to(strip, (pos, 2 * pos))
            strip = pltpu.roll(strip, 1, 1, stride=1, stride_axis=0)
            bias[head, block] = strip[:, :pos].astype(bf16)

    for step in (1, 2):
        for row in range(2):
            for way in range(2):
                pl.when(receives(way, step))(
                    lambda way=way, step=step, row=row: hop(way, step, row).wait_recv()
                )
                pl.when(sends(way, step + 1))(
                    lambda way=way, step=step, row=row: hop(way, step + 1, row).start()
                )
    cot_x.wait_recv()
    cot_far = links.send(cot_near.at[t], cot_near.at[t], links.core)
    for row in range(2):
        for way in range(2):
            pl.when(receives(way, 3))(lambda way=way, row=row: hop(way, 3, row).wait_recv())

    def attend(row, carry):
        seg_query = seg_rows[row, :, pl.ds(pl.multiple_of(s * pos, 128), pos)]
        same = []
        for block in range(4):
            seg_key = seg_rows[row, :, block * pos : (block + 1) * pos]
            same.append(jnp.broadcast_to(seg_key, (pos, pos)).T == seg_query)
        parts = []
        for head in range(heads):
            lanes = slice(head * dh, (head + 1) * dh)
            lanes_v = slice(inner + head * dh, inner + (head + 1) * dh)
            query = queries[row, :, lanes]
            scores = [
                jnp.where(
                    same[block],
                    dot_f32(pairs[block, row, :, lanes], query, NT) + bias[head, block].astype(f32),
                    masked_score,
                )
                for block in range(4)
            ]
            top = jnp.max(scores[0], axis=0, keepdims=True)
            for block in range(1, 4):
                top = jnp.maximum(top, jnp.max(scores[block], axis=0, keepdims=True))
            total = jnp.zeros_like(top)
            mixed = jnp.zeros((dh, pos), f32)
            for block in range(4):
                grown = jnp.exp(scores[block] - top)
                total = total + jnp.sum(grown, axis=0, keepdims=True)
                mixed = mixed + dot_f32(pairs[block, row, :, lanes_v], grown.astype(bf16), TN)
            log_total[row, head : head + 1] = top + jnp.log(total)
            parts.append(mixed * (1.0 / total))
        context[row] = jnp.concatenate(parts, axis=0).T.astype(bf16)
        return carry

    lax.fori_loop(0, rows, attend, 0)

    send_buf[...] = dot_f32(context[1 - t], w_out[...], NT).astype(bf16)
    branch_core = links.send(send_buf, recv_buf, links.core)
    branch = dot_f32(context[t], w_out[...], NT)
    branch_core.wait_recv()
    values = tokens[...].astype(f32) + (branch + recv_buf[...].astype(f32))
    after_attn[...] = values
    ff_pair[t] = (values * unit_scale(values) * gain_ff[...]).astype(bf16)
    ff_core = links.send(ff_pair.at[t], ff_pair.at[t], links.core)
    ff_core.wait_recv()
    cot_core.wait_recv()
    cot_far.wait_recv()
    own_cot.wait()
    links.finish()
    for step in (1, 2, 3):
        for row in range(2):
            for way in range(2):
                pl.when(sends(way, step))(
                    lambda way=way, step=step, row=row: hop(way, step, row).wait_send()
                )


def vmem_spec():
    return pl.BlockSpec(memory_space=pltpu.VMEM)


def forward_part(tokens, cotangent, seg_rows, bucket_window, table_t, gain_attn, gain_ff, w_query, w_key, w_value, w_out):
    pos, width = tokens.shape
    inner = w_query.shape[1]
    heads = 3
    shape = jax.ShapeDtypeStruct
    outs = (
        shape((2, pos, width), bf16),
        shape((2, pos, inner), bf16),
        shape((4, 2, pos, 2 * inner), bf16),
        shape((2, pos, inner), bf16),
        shape((2, heads, pos), f32),
        shape((pos, width), f32),
        shape((2, pos, width), bf16),
        shape((2, pos, width), bf16),
        shape((2, pos, width), bf16),
        shape((heads, 4, pos, pos), bf16),
    )
    return pl.pallas_call(
        forward_kernel,
        out_shape=outs,
        in_specs=[vmem_spec()] * 11,
        out_specs=tuple(vmem_spec() for _ in outs),
        scratch_shapes=[
            pltpu.VMEM((8, 2048), f32),
            pltpu.VMEM((pos, width), bf16),
            pltpu.VMEM((pos, width), bf16),
            pltpu.SemaphoreType.DMA,
            pltpu.SemaphoreType.DMA((20,)),
            pltpu.SemaphoreType.DMA((20,)),
        ],
        compiler_params=pltpu.CompilerParams(
            collective_id=1, has_side_effects=True, vmem_limit_bytes=56 * 2**20
        ),
        name="forward_part",
    )(tokens, cotangent, seg_rows, bucket_window, table_t, gain_attn, gain_ff, w_query, w_key, w_value, w_out)


def shards(
    tokens,
    segment_ids,
    buckets,
    gain_attn,
    w_query,
    w_key,
    w_value,
    w_out,
    rel_table,
    gain_ff,
    w_gate,
    w_up,
    w_down,
    cotangent,
):
    rows_dev, pos_dev, width = tokens.shape
    length = pos_dev * lax.axis_size("seq")
    query_start = lax.axis_index("seq") * pos_dev
    num_buckets, heads_dev = rel_table.shape
    inner_dev = w_query.shape[1]
    head_dim = inner_dev // heads_dev
    window_len = length + pos_dev - 1
    window_start = length - pos_dev - query_start
    tokens_f = tokens.astype(jnp.float32)
    normed_attn, norm_attn_back = jax.vjp(rms_scale, tokens_f, gain_attn.astype(jnp.float32))
    bwin = jnp.pad(jnp.flip(buckets), (0, 1))[None]
    table_t = jnp.pad(rel_table.T, ((0, 5), (0, 0)))
    attn_rows, queries, kv_all, context_low, lse, aa, ff_rows0, grad_rows_ff, cot_near, biasT = forward_part(
        tokens[0], cotangent[0], segment_ids[:, None, :], bwin, table_t, gain_attn.astype(jnp.float32)[None], gain_ff.astype(jnp.float32)[None], w_query, w_key, w_value, w_out)
    group_rows = 2
    bucket_ids = jnp.arange(num_buckets, dtype=jnp.int32)
    log_total = lse[..., None]
    context = context_low.astype(jnp.float32).reshape(2, pos_dev, heads_dev, head_dim)
    kvt = kv_all.transpose(1, 0, 2, 3).reshape(2, length, 384)
    pairs_all = jnp.stack([kvt[..., :192], kvt[..., 192:]], 1)
    query_heads = queries.reshape(group_rows, pos_dev, heads_dev, head_dim)
    key_heads = pairs_all[:, 0].reshape(group_rows, length, heads_dev, head_dim)
    value_heads = pairs_all[:, 1].reshape(group_rows, length, heads_dev, head_dim)
    pos_bias = biasT.reshape(3, length, pos_dev).transpose(0, 2, 1).astype(jnp.float32)
    seg_query = lax.dynamic_slice_in_dim(segment_ids, query_start, pos_dev, 1)
    same_doc = seg_query[:, None, :, None] == segment_ids[:, None, None, :]

    def score_rows():
        raw_scores = jnp.einsum(
            "rqhd,rkhd->rhqk", query_heads, key_heads, preferred_element_type=jnp.float32
        )
        return jnp.where(same_doc, raw_scores + pos_bias[None], masked_score)
    after_attn = aa[None]
    normed_ff, norm_ff_back = jax.vjp(rms_scale, after_attn, gain_ff.astype(jnp.float32))
    shard_rows = ff_rows0
    gate_pre = jnp.dot(shard_rows, w_gate, preferred_element_type=jnp.float32)
    up_pre = jnp.dot(shard_rows, w_up, preferred_element_type=jnp.float32)
    ff_rows, gate_pre, up_pre = (shard_rows, gate_pre, up_pre)
    hidden, hidden_back = jax.vjp(gated_unit, gate_pre, up_pre)
    hidden_low = hidden.astype(jnp.bfloat16)
    ff_branch = lax.psum_scatter(
        times_weight_t(hidden_low, w_down).astype(jnp.bfloat16),
        "tensor",
        scatter_dimension=0,
        tiled=True,
    ).astype(jnp.float32)
    layer_out = after_attn + ff_branch
    shard_rows = grad_rows_ff
    grad_hidden = jnp.dot(shard_rows, w_down, preferred_element_type=jnp.float32)
    grad_w_down = token_sum(grad_rows_ff, hidden_low)
    grad_gate, grad_up = hidden_back(grad_hidden)
    grad_gate = grad_gate.astype(jnp.bfloat16)
    grad_up = grad_up.astype(jnp.bfloat16)
    grad_normed_ff = lax.psum_scatter(
        (times_weight_t(grad_gate, w_gate) + times_weight_t(grad_up, w_up)).astype(jnp.bfloat16),
        "tensor",
        scatter_dimension=0,
        tiled=True,
    ).astype(jnp.float32)
    grad_w_gate = token_sum(ff_rows, grad_gate)
    grad_w_up = token_sum(ff_rows, grad_up)
    grad_mid_norm, grad_gain_ff_local = norm_ff_back(grad_normed_ff)
    grad_after_attn = cotangent.astype(jnp.float32) + grad_mid_norm
    grad_branch = grad_after_attn.astype(jnp.bfloat16)
    shard_rows = lax.all_gather(grad_branch, "tensor", axis=0, tiled=True)
    grad_context = jnp.dot(shard_rows, w_out, preferred_element_type=jnp.float32).astype(
        jnp.bfloat16
    )
    grad_w_out = token_sum(shard_rows, context_low)
    probs_again = jnp.exp(score_rows() - log_total)
    grad_ctx_heads = grad_context.reshape(group_rows, pos_dev, heads_dev, head_dim)
    grad_probs = jnp.einsum(
        "rqhd,rkhd->rhqk", grad_ctx_heads, value_heads, preferred_element_type=jnp.float32
    )
    row_delta = jnp.einsum("rqhd,rqhd->rhq", grad_ctx_heads.astype(jnp.float32), context)
    grad_scores = (probs_again * (grad_probs - row_delta[..., None])).astype(jnp.bfloat16)
    probs_low = probs_again.astype(jnp.bfloat16)
    grad_queries = jnp.einsum(
        "rhqk,rkhd->rqhd", grad_scores, key_heads, preferred_element_type=jnp.float32
    )
    grad_queries = grad_queries.reshape(group_rows, pos_dev, inner_dev).astype(jnp.bfloat16)
    grad_key_part = jnp.einsum(
        "rhqk,rqhd->rkhd", grad_scores, query_heads, preferred_element_type=jnp.float32
    )
    grad_value_part = jnp.einsum(
        "rhqk,rqhd->rkhd", probs_low, grad_ctx_heads, preferred_element_type=jnp.float32
    )
    grad_key_part = grad_key_part.reshape(group_rows, length, inner_dev)
    grad_value_part = grad_value_part.reshape(group_rows, length, inner_dev)
    grad_keys, grad_values = (
        lax.psum_scatter(
            grad_key_part.astype(jnp.bfloat16), "seq", scatter_dimension=1, tiled=True
        ).astype(jnp.float32),
        lax.psum_scatter(
            grad_value_part.astype(jnp.bfloat16), "seq", scatter_dimension=1, tiled=True
        ).astype(jnp.float32),
    )
    grad_keys = grad_keys.astype(jnp.bfloat16)
    grad_values = grad_values.astype(jnp.bfloat16)
    table_window = diagonal_sums(jnp.sum(grad_scores.astype(jnp.float32), axis=0))
    window_ids = lax.dynamic_slice_in_dim(buckets, window_start, window_len, 0)
    window_hot = (window_ids[:, None] == bucket_ids[None, :]).astype(jnp.float32)
    grad_table_local = lax.dot_general(
        window_hot,
        table_window,
        (((0,), (1,)), ((), ())),
        precision=highest,
        preferred_element_type=jnp.float32,
    )
    grad_normed_attn = lax.psum_scatter(
        (
            times_weight_t(grad_queries, w_query)
            + times_weight_t(grad_keys, w_key)
            + times_weight_t(grad_values, w_value)
        ).astype(jnp.bfloat16),
        "tensor",
        scatter_dimension=0,
        tiled=True,
    ).astype(jnp.float32)
    grad_w_query = token_sum(attn_rows, grad_queries)
    grad_w_key = token_sum(attn_rows, grad_keys)
    grad_w_value = token_sum(attn_rows, grad_values)
    grad_tokens_norm, grad_gain_attn_local = norm_attn_back(grad_normed_attn)
    grad_tokens = grad_after_attn + grad_tokens_norm
    table_full = jnp.zeros((num_buckets, heads_dev * lax.axis_size("tensor")), jnp.float32)
    table_full = lax.dynamic_update_slice_in_dim(
        table_full, grad_table_local, lax.axis_index("tensor") * heads_dev, 1
    )
    grad_gain_attn, grad_gain_ff, grad_rel_table = lax.psum(
        (grad_gain_attn_local, grad_gain_ff_local, table_full), ("dp", "tensor", "seq")
    )
    weight_grads = (
        grad_w_query,
        grad_w_key,
        grad_w_value,
        grad_w_out,
        grad_w_gate,
        grad_w_up,
        grad_w_down,
    )
    col_counts = [single.shape[1] for single in weight_grads]
    flat_parts = jax.tree.map(
        lambda part: part.astype(jnp.float32),
        lax.psum_scatter(
            shortened(tuple((single.reshape(-1) for single in weight_grads))),
            "dp",
            scatter_dimension=0,
            tiled=True,
        ),
    )
    shaped_parts = tuple((flat_parts[place].reshape(-1, col_counts[place]) for place in range(7)))
    done_q, done_k, done_v, done_o, done_g, done_u, done_d = jax.tree.map(
        lambda part: part.astype(jnp.float32),
        lax.psum_scatter(shortened(shaped_parts), "seq", scatter_dimension=1, tiled=True),
    )
    return (
        layer_out,
        grad_tokens,
        grad_gain_attn,
        done_q,
        done_k,
        done_v,
        done_o,
        grad_rel_table,
        grad_gain_ff,
        done_g,
        done_u,
        done_d,
    )


def solution(mesh):
    return jax.shard_map(
        shards,
        mesh=mesh,
        in_specs=(
            P(("dp", "tensor"), "seq", None),
            P("dp", None),
            P(),
            P(),
            P(None, "tensor"),
            P(None, "tensor"),
            P(None, "tensor"),
            P(None, "tensor"),
            P(None, "tensor"),
            P(),
            P(None, "tensor"),
            P(None, "tensor"),
            P(None, "tensor"),
            P(("dp", "tensor"), "seq", None),
        ),
        out_specs=(
            P(("dp", "tensor"), "seq", None),
            P(("dp", "tensor"), "seq", None),
            P(),
            P("dp", ("tensor", "seq")),
            P("dp", ("tensor", "seq")),
            P("dp", ("tensor", "seq")),
            P("dp", ("tensor", "seq")),
            P(),
            P(),
            P("dp", ("tensor", "seq")),
            P("dp", ("tensor", "seq")),
            P("dp", ("tensor", "seq")),
        ),
        check_vma=False,
    )
```

```python
import math

import jax
import jax.numpy as jnp
from jax import lax
from jax.experimental import pallas as pl
from jax.experimental.pallas import tpu as pltpu
from jax.sharding import PartitionSpec as P

eps_norm = 1e-06
gelu_scale = math.sqrt(2.0 / math.pi)
masked_score = -1e30
highest = lax.Precision.HIGHEST


def shortened(shard):

    def short(part):
        return part.astype(jnp.bfloat16) if part.dtype == jnp.float32 else part

    return jax.tree.map(short, shard)


def gelu_tanh(values):
    return (
        0.5 * values * (1.0 + jnp.tanh(gelu_scale * (values + 0.044715 * values * values * values)))
    )


def rms_scale(values, gain_vec):
    return (
        values * lax.rsqrt(jnp.mean(values * values, axis=-1, keepdims=True) + eps_norm) * gain_vec
    )


def gated_unit(gate_pre, up_pre):
    return gelu_tanh(gate_pre) * up_pre


def token_sum(left, right):
    left_flat = left.reshape(-1, left.shape[-1])
    right_flat = right.reshape(-1, right.shape[-1])
    return lax.dot_general(
        left_flat, right_flat, (((0,), (0,)), ((), ())), preferred_element_type=jnp.float32
    )


def times_weight_t(values, weight):
    return lax.dot_general(
        values, weight, (((values.ndim - 1,), (1,)), ((), ())), preferred_element_type=jnp.float32
    )


def toeplitz_rows(window, row_count, col_count):
    window_len = window.shape[1]
    turned = jnp.roll(window, -(row_count - 1), axis=1)
    repeated = jnp.tile(turned, (1, row_count))[:, : row_count * (window_len - 1)]
    return repeated.reshape(window.shape[0], row_count, window_len - 1)[:, :, :col_count]


def diagonal_sums(score_block):
    head_count, row_count, col_count = score_block.shape
    flipped = jnp.flip(score_block, axis=1)
    padded = jnp.pad(flipped, ((0, 0), (0, 0), (0, row_count)))
    sheared = padded.reshape(head_count, row_count * (col_count + row_count))
    sheared = sheared[:, : row_count * (col_count + row_count - 1)]
    return jnp.sum(sheared.reshape(head_count, row_count, col_count + row_count - 1), axis=1)


def shards(
    tokens,
    segment_ids,
    buckets,
    gain_attn,
    w_query,
    w_key,
    w_value,
    w_out,
    rel_table,
    gain_ff,
    w_gate,
    w_up,
    w_down,
    cotangent,
):
    rows_dev, pos_dev, width = tokens.shape
    length = pos_dev * lax.axis_size("seq")
    query_start = lax.axis_index("seq") * pos_dev
    num_buckets, heads_dev = rel_table.shape
    inner_dev = w_query.shape[1]
    head_dim = inner_dev // heads_dev
    window_len = length + pos_dev - 1
    window_start = length - pos_dev - query_start
    tokens_f = tokens.astype(jnp.float32)
    normed_attn, norm_attn_back = jax.vjp(rms_scale, tokens_f, gain_attn.astype(jnp.float32))
    normed_attn = normed_attn.astype(jnp.bfloat16)
    w_pair = jnp.stack((w_key, w_value))
    shard_rows = lax.all_gather(normed_attn, "tensor", axis=0, tiled=True)
    queries = jnp.dot(shard_rows, w_query, preferred_element_type=jnp.float32).astype(jnp.bfloat16)
    pairs = jnp.einsum(
        "rcd,sde->rsce", shard_rows, w_pair, preferred_element_type=jnp.float32
    ).astype(jnp.bfloat16)
    attn_rows, queries, pairs = (shard_rows, queries, pairs)
    pairs_all = lax.all_gather(pairs, "seq", axis=2, tiled=True)
    group_rows = attn_rows.shape[0]
    bucket_ids = jnp.arange(num_buckets, dtype=jnp.int32)
    one_hot_all = (buckets[:, None] == bucket_ids[None, :]).astype(jnp.bfloat16)
    per_offset = jnp.dot(one_hot_all, rel_table, preferred_element_type=jnp.float32)
    window = lax.dynamic_slice_in_dim(per_offset, window_start, window_len, 0)
    pos_bias = toeplitz_rows(window.T, pos_dev, length)
    seg_query = lax.dynamic_slice_in_dim(segment_ids, query_start, pos_dev, 1)
    same_doc = seg_query[:, None, :, None] == segment_ids[:, None, None, :]
    query_heads = queries.reshape(group_rows, pos_dev, heads_dev, head_dim)
    key_heads = pairs_all[:, 0].reshape(group_rows, length, heads_dev, head_dim)
    value_heads = pairs_all[:, 1].reshape(group_rows, length, heads_dev, head_dim)

    def score_rows():
        raw_scores = jnp.einsum(
            "rqhd,rkhd->rhqk", query_heads, key_heads, preferred_element_type=jnp.float32
        )
        return jnp.where(same_doc, raw_scores + pos_bias[None], masked_score)

    scores = score_rows()
    row_max = jnp.max(scores, axis=-1, keepdims=True)
    exp_scores = jnp.exp(scores - row_max)
    row_total = jnp.sum(exp_scores, axis=-1, keepdims=True)
    attn_probs = (exp_scores / row_total).astype(jnp.bfloat16)
    log_total = row_max + jnp.log(row_total)
    context = jnp.einsum(
        "rhqk,rkhd->rqhd", attn_probs, value_heads, preferred_element_type=jnp.float32
    )
    context_low = context.reshape(group_rows, pos_dev, inner_dev).astype(jnp.bfloat16)
    attn_branch = lax.psum_scatter(
        times_weight_t(context_low, w_out).astype(jnp.bfloat16),
        "tensor",
        scatter_dimension=0,
        tiled=True,
    ).astype(jnp.float32)
    after_attn = tokens_f + attn_branch
    normed_ff, norm_ff_back = jax.vjp(rms_scale, after_attn, gain_ff.astype(jnp.float32))
    normed_ff = normed_ff.astype(jnp.bfloat16)
    shard_rows = lax.all_gather(normed_ff, "tensor", axis=0, tiled=True)
    gate_pre = jnp.dot(shard_rows, w_gate, preferred_element_type=jnp.float32)
    up_pre = jnp.dot(shard_rows, w_up, preferred_element_type=jnp.float32)
    ff_rows, gate_pre, up_pre = (shard_rows, gate_pre, up_pre)
    hidden, hidden_back = jax.vjp(gated_unit, gate_pre, up_pre)
    hidden_low = hidden.astype(jnp.bfloat16)
    ff_branch = lax.psum_scatter(
        times_weight_t(hidden_low, w_down).astype(jnp.bfloat16),
        "tensor",
        scatter_dimension=0,
        tiled=True,
    ).astype(jnp.float32)
    layer_out = after_attn + ff_branch
    shard_rows = lax.all_gather(cotangent, "tensor", axis=0, tiled=True)
    grad_rows_ff = shard_rows
    grad_hidden = jnp.dot(shard_rows, w_down, preferred_element_type=jnp.float32)
    grad_w_down = token_sum(grad_rows_ff, hidden_low)
    grad_gate, grad_up = hidden_back(grad_hidden)
    grad_gate = grad_gate.astype(jnp.bfloat16)
    grad_up = grad_up.astype(jnp.bfloat16)
    grad_normed_ff = lax.psum_scatter(
        (times_weight_t(grad_gate, w_gate) + times_weight_t(grad_up, w_up)).astype(jnp.bfloat16),
        "tensor",
        scatter_dimension=0,
        tiled=True,
    ).astype(jnp.float32)
    grad_w_gate = token_sum(ff_rows, grad_gate)
    grad_w_up = token_sum(ff_rows, grad_up)
    grad_mid_norm, grad_gain_ff_local = norm_ff_back(grad_normed_ff)
    grad_after_attn = cotangent.astype(jnp.float32) + grad_mid_norm
    grad_branch = grad_after_attn.astype(jnp.bfloat16)
    shard_rows = lax.all_gather(grad_branch, "tensor", axis=0, tiled=True)
    grad_context = jnp.dot(shard_rows, w_out, preferred_element_type=jnp.float32).astype(
        jnp.bfloat16
    )
    grad_w_out = token_sum(shard_rows, context_low)
    probs_again = jnp.exp(score_rows() - log_total)
    grad_ctx_heads = grad_context.reshape(group_rows, pos_dev, heads_dev, head_dim)
    grad_probs = jnp.einsum(
        "rqhd,rkhd->rhqk", grad_ctx_heads, value_heads, preferred_element_type=jnp.float32
    )
    row_delta = jnp.einsum("rqhd,rqhd->rhq", grad_ctx_heads.astype(jnp.float32), context)
    grad_scores = (probs_again * (grad_probs - row_delta[..., None])).astype(jnp.bfloat16)
    probs_low = probs_again.astype(jnp.bfloat16)
    grad_queries = jnp.einsum(
        "rhqk,rkhd->rqhd", grad_scores, key_heads, preferred_element_type=jnp.float32
    )
    grad_queries = grad_queries.reshape(group_rows, pos_dev, inner_dev).astype(jnp.bfloat16)
    grad_key_part = jnp.einsum(
        "rhqk,rqhd->rkhd", grad_scores, query_heads, preferred_element_type=jnp.float32
    )
    grad_value_part = jnp.einsum(
        "rhqk,rqhd->rkhd", probs_low, grad_ctx_heads, preferred_element_type=jnp.float32
    )
    grad_key_part = grad_key_part.reshape(group_rows, length, inner_dev)
    grad_value_part = grad_value_part.reshape(group_rows, length, inner_dev)
    grad_keys, grad_values = (
        lax.psum_scatter(
            grad_key_part.astype(jnp.bfloat16), "seq", scatter_dimension=1, tiled=True
        ).astype(jnp.float32),
        lax.psum_scatter(
            grad_value_part.astype(jnp.bfloat16), "seq", scatter_dimension=1, tiled=True
        ).astype(jnp.float32),
    )
    grad_keys = grad_keys.astype(jnp.bfloat16)
    grad_values = grad_values.astype(jnp.bfloat16)
    table_window = diagonal_sums(jnp.sum(grad_scores.astype(jnp.float32), axis=0))
    window_ids = lax.dynamic_slice_in_dim(buckets, window_start, window_len, 0)
    window_hot = (window_ids[:, None] == bucket_ids[None, :]).astype(jnp.float32)
    grad_table_local = lax.dot_general(
        window_hot,
        table_window,
        (((0,), (1,)), ((), ())),
        precision=highest,
        preferred_element_type=jnp.float32,
    )
    grad_normed_attn = lax.psum_scatter(
        (
            times_weight_t(grad_queries, w_query)
            + times_weight_t(grad_keys, w_key)
            + times_weight_t(grad_values, w_value)
        ).astype(jnp.bfloat16),
        "tensor",
        scatter_dimension=0,
        tiled=True,
    ).astype(jnp.float32)
    grad_w_query = token_sum(attn_rows, grad_queries)
    grad_w_key = token_sum(attn_rows, grad_keys)
    grad_w_value = token_sum(attn_rows, grad_values)
    grad_tokens_norm, grad_gain_attn_local = norm_attn_back(grad_normed_attn)
    grad_tokens = grad_after_attn + grad_tokens_norm
    table_full = jnp.zeros((num_buckets, heads_dev * lax.axis_size("tensor")), jnp.float32)
    table_full = lax.dynamic_update_slice_in_dim(
        table_full, grad_table_local, lax.axis_index("tensor") * heads_dev, 1
    )
    grad_gain_attn, grad_gain_ff, grad_rel_table = lax.psum(
        (grad_gain_attn_local, grad_gain_ff_local, table_full), ("dp", "tensor", "seq")
    )
    weight_grads = (
        grad_w_query,
        grad_w_key,
        grad_w_value,
        grad_w_out,
        grad_w_gate,
        grad_w_up,
        grad_w_down,
    )
    col_counts = [single.shape[1] for single in weight_grads]
    flat_parts = jax.tree.map(
        lambda part: part.astype(jnp.float32),
        lax.psum_scatter(
            shortened(tuple((single.reshape(-1) for single in weight_grads))),
            "dp",
            scatter_dimension=0,
            tiled=True,
        ),
    )
    shaped_parts = tuple((flat_parts[place].reshape(-1, col_counts[place]) for place in range(7)))
    done_q, done_k, done_v, done_o, done_g, done_u, done_d = jax.tree.map(
        lambda part: part.astype(jnp.float32),
        lax.psum_scatter(shortened(shaped_parts), "seq", scatter_dimension=1, tiled=True),
    )
    return (
        layer_out,
        grad_tokens,
        grad_gain_attn,
        done_q,
        done_k,
        done_v,
        done_o,
        grad_rel_table,
        grad_gain_ff,
        done_g,
        done_u,
        done_d,
    )


f32, bf16 = jnp.float32, jnp.bfloat16
MESH = pl.DeviceIdType.MESH
NT = (((1,), (1,)), ((), ()))
TN = (((0,), (0,)), ((), ()))


def dot_f32(left, right, dims=(((1,), (0,)), ((), ()))):
    return lax.dot_general(left, right, dims, preferred_element_type=f32)


class Links:
    def __init__(self, send_sems, recv_sems):
        self.send_sems, self.recv_sems, self.count, self.open = send_sems, recv_sems, 0, []
        dp, core, seq = lax.axis_index("dp"), lax.axis_index("tensor"), lax.axis_index("seq")
        self.dp, self.t, self.s = dp, core, seq
        self.x = lax.rem(dp, 2)
        self.y = lax.div(dp, 2)
        self.core = (dp, 1 - core, seq)
        self.xdev = (dp + 1 - 2 * self.x, core, seq)
        self.ydev = (dp + 2 - 4 * self.y, core, seq)

    def z(self, step):
        return (self.dp, self.t, lax.rem(self.s + step + 4, 4))

    def to_seq(self, target):
        return (self.dp, self.t, target)

    def slots(self, amount=1):
        first = self.count
        self.count += amount
        return first

    def copy(self, src, dst, device, slot=None):
        slot = self.slots() if slot is None else slot
        return pltpu.make_async_remote_copy(
            src_ref=src,
            dst_ref=dst,
            send_sem=self.send_sems.at[slot],
            recv_sem=self.recv_sems.at[slot],
            device_id=device,
            device_id_type=MESH,
        )

    def send(self, src, dst, device):
        single = self.copy(src, dst, device)
        single.start()
        self.open.append(single)
        return single

    def sent(self, single):
        single.wait_send()
        self.open = [other for other in self.open if other is not single]

    def finish(self):
        for single in self.open:
            single.wait_send()
        self.open = []

    def greet(self, devices):
        barrier = pltpu.get_barrier_semaphore()
        for device in devices:
            pl.semaphore_signal(barrier, inc=1, device_id=device, device_id_type=MESH)
        pl.semaphore_wait(barrier, len(devices))


def unit_scale(values):
    return lax.rsqrt(jnp.mean(values * values, axis=-1, keepdims=True) + eps_norm)


def forward_kernel(
    tokens,
    cotangent,
    seg_rows,
    bucket_window,
    table_t,
    gain_attn,
    gain_ff,
    w_query,
    w_key,
    w_value,
    w_out,
    normed_pair,
    queries,
    pairs,
    context,
    log_total,
    after_attn,
    ff_pair,
    cot_pair,
    cot_near,
    bias,
    per_offset,
    send_buf,
    recv_buf,
    local_sem,
    send_sems,
    recv_sems,
):
    links = Links(send_sems, recv_sems)
    t, s = links.t, links.s
    rows, pos, width = normed_pair.shape
    inner = queries.shape[2]
    heads = log_total.shape[1]
    dh = inner // heads
    links.greet([links.core, links.xdev, links.z(1), links.z(2), links.z(3)])
    own_cot = pltpu.make_async_copy(cotangent, cot_pair.at[t], local_sem)
    own_cot.start()
    cot_core = links.send(cotangent, cot_pair.at[t], links.core)
    cot_x = links.send(cotangent, cot_near.at[t], links.xdev)

    values = tokens[...].astype(f32)
    normed_pair[t] = (values * unit_scale(values) * gain_attn[...]).astype(bf16)
    normed_core = links.send(normed_pair.at[t], normed_pair.at[t], links.core)

    chain = links.slots(2 * 3 * 2)

    def hop(way, step, row):
        slot = chain + (way * 3 + step - 1) * 2 + row
        step_by = 1 if way == 0 else -1
        block = lax.rem(s - step_by * (step - 1) + 4, 4)
        place = lax.rem(t + row, 2)
        return links.copy(
            pairs.at[block, place], pairs.at[block, place], links.z(step_by), slot
        )

    def sends(way, step):
        return (s >= step - 1) & (s < 3) if way == 0 else (s <= 4 - step) & (s > 0)

    def receives(way, step):
        return s >= step if way == 0 else s <= 3 - step

    def project(place, row):
        block = normed_pair[place]
        queries[place] = dot_f32(block, w_query[...]).astype(bf16)
        pairs[s, place] = jnp.concatenate(
            [dot_f32(block, w_key[...]), dot_f32(block, w_value[...])], axis=1
        ).astype(bf16)
        for way in range(2):
            pl.when(sends(way, 1))(lambda way=way: hop(way, 1, row).start())

    project(t, 0)
    normed_core.wait_recv()
    project(1 - t, 1)

    bucket_ids = lax.broadcasted_iota(jnp.int32, (table_t.shape[1], bucket_window.shape[1]), 0)
    one_hot = (bucket_ids == bucket_window[...]).astype(bf16)
    per_offset[...] = dot_f32(table_t[...], one_hot)
    window = per_offset[:, pl.ds(pl.multiple_of(s * pos, 128), 5 * pos)]
    for head in range(heads):
        for block in range(4):
            strip = jnp.concatenate(
                [
                    window[head : head + 1, (4 - block) * pos : (5 - block) * pos],
                    window[head : head + 1, (3 - block) * pos : (4 - block) * pos],
                ],
                axis=1,
            )
            strip = jnp.broadcast_to(strip, (pos, 2 * pos))
            strip = pltpu.roll(strip, 1, 1, stride=1, stride_axis=0)
            bias[(head * 4 + block) * pos : (head * 4 + block + 1) * pos, :] = strip[:, :pos].astype(bf16)

    for step in (1, 2):
        for row in range(2):
            for way in range(2):
                pl.when(receives(way, step))(
                    lambda way=way, step=step, row=row: hop(way, step, row).wait_recv()
                )
                pl.when(sends(way, step + 1))(
                    lambda way=way, step=step, row=row: hop(way, step + 1, row).start()
                )
    cot_x.wait_recv()
    cot_far = links.send(cot_near.at[t], cot_near.at[t], links.core)
    for row in range(2):
        for way in range(2):
            pl.when(receives(way, 3))(lambda way=way, row=row: hop(way, 3, row).wait_recv())

    def attend(row, carry):
        seg_query = seg_rows[row, :, pl.ds(pl.multiple_of(s * pos, 128), pos)]
        same = []
        for block in range(4):
            seg_key = seg_rows[row, :, block * pos : (block + 1) * pos]
            same.append(jnp.broadcast_to(seg_key, (pos, pos)).T == seg_query)
        parts = []
        for head in range(heads):
            lanes = slice(head * dh, (head + 1) * dh)
            lanes_v = slice(inner + head * dh, inner + (head + 1) * dh)
            query = queries[row, :, lanes]
            scores = [
                jnp.where(
                    same[block],
                    dot_f32(pairs[block, row, :, lanes], query, NT)
                    + bias[(head * 4 + block) * pos : (head * 4 + block + 1) * pos, :].astype(f32),
                    masked_score,
                )
                for block in range(4)
            ]
            top = jnp.max(scores[0], axis=0, keepdims=True)
            for block in range(1, 4):
                top = jnp.maximum(top, jnp.max(scores[block], axis=0, keepdims=True))
            total = jnp.zeros_like(top)
            mixed = jnp.zeros((dh, pos), f32)
            for block in range(4):
                grown = jnp.exp(scores[block] - top)
                total = total + jnp.sum(grown, axis=0, keepdims=True)
                mixed = mixed + dot_f32(pairs[block, row, :, lanes_v], grown.astype(bf16), TN)
            log_total[row, head : head + 1] = top + jnp.log(total)
            parts.append(mixed * (1.0 / total))
        context[row] = jnp.concatenate(parts, axis=0).T
        return carry

    lax.fori_loop(0, rows, attend, 0)

    send_buf[...] = dot_f32(context[1 - t].astype(bf16), w_out[...], NT).astype(bf16)
    branch_core = links.send(send_buf, recv_buf, links.core)
    branch = dot_f32(context[t].astype(bf16), w_out[...], NT)
    branch_core.wait_recv()
    values = tokens[...].astype(f32) + (branch + recv_buf[...].astype(f32))
    after_attn[...] = values
    ff_pair[t] = (values * unit_scale(values) * gain_ff[...]).astype(bf16)
    ff_core = links.send(ff_pair.at[t], ff_pair.at[t], links.core)
    ff_core.wait_recv()
    cot_core.wait_recv()
    cot_far.wait_recv()
    own_cot.wait()
    links.finish()
    for step in (1, 2, 3):
        for row in range(2):
            for way in range(2):
                pl.when(sends(way, step))(
                    lambda way=way, step=step, row=row: hop(way, step, row).wait_send()
                )


def vmem_spec():
    return pl.BlockSpec(memory_space=pltpu.VMEM)


def forward_part(tokens, cotangent, seg_rows, bucket_window, table_t, gain_attn, gain_ff, w_query, w_key, w_value, w_out):
    pos, width = tokens.shape
    inner = w_query.shape[1]
    heads = 3
    shape = jax.ShapeDtypeStruct
    outs = (
        shape((2, pos, width), bf16),
        shape((2, pos, inner), bf16),
        shape((4, 2, pos, 2 * inner), bf16),
        shape((2, pos, inner), f32),
        shape((2, heads, pos), f32),
        shape((pos, width), f32),
        shape((2, pos, width), bf16),
        shape((2, pos, width), bf16),
        shape((2, pos, width), bf16),
        shape((heads * 4 * pos, pos), bf16),
    )
    return pl.pallas_call(
        forward_kernel,
        out_shape=outs,
        in_specs=[vmem_spec()] * 11,
        out_specs=tuple(vmem_spec() for _ in outs),
        scratch_shapes=[
            pltpu.VMEM((8, 2048), f32),
            pltpu.VMEM((pos, width), bf16),
            pltpu.VMEM((pos, width), bf16),
            pltpu.SemaphoreType.DMA,
            pltpu.SemaphoreType.DMA((20,)),
            pltpu.SemaphoreType.DMA((20,)),
        ],
        compiler_params=pltpu.CompilerParams(
            collective_id=1, has_side_effects=True, vmem_limit_bytes=56 * 2**20
        ),
        name="forward_part",
    )(tokens, cotangent, seg_rows, bucket_window, table_t, gain_attn, gain_ff, w_query, w_key, w_value, w_out)


row_parts = ((0, 96), (96, 96), (192, 96), (288, 80))


def backward_kernel(
    w_gate,
    w_up,
    w_down,
    w_small,
    normed_pair,
    tokens,
    queries,
    pairs_in,
    context,
    log_total,
    after_in,
    ff_in,
    cot_in,
    near_in,
    bias_in,
    seg_rows,
    bucket_window,
    gain_attn,
    gain_ff,
    layer_out,
    grad_tokens,
    out_big,
    out_small,
    out_vec,
    big,
    acts,
    ff_t,
    cot_t,
    ff_own,
    ff_near,
    cot_own,
    cot_near,
    after_attn,
    mid,
    spare,
    y_recv,
    za_recv,
    zb_recv,
    stage,
    kv_za_recv,
    kv_zb_recv,
    gx_recv,
    gy_send,
    g_keep,
    gy_recv,
    gza_recv,
    gzb_send,
    gzb_recv,
    core_send,
    core_recv,
    grad_q,
    grad_ctx,
    diag,
    vec,
    vec_recv,
    load_sems,
    out_sems,
    send_sems,
    recv_sems,
):
    links = Links(send_sems, recv_sems)
    t, s, x, y = links.t, links.s, links.x, links.y
    pos, width = after_attn.shape
    hidden = big.shape[2]
    half = hidden // 2
    quarter = hidden // 4
    block_rows = y_recv.shape[1]
    inner = queries.shape[2]
    heads = bias_in.shape[0] // (4 * pos)
    dh = inner // heads
    kv_first = 1536
    pair_mate = s + 1 - 2 * lax.rem(s, 2)
    keep_half = lax.rem(s, 2)
    send_half = 1 - keep_half
    inside = (s >= 1) & (s <= 2)
    first_to = 1 + lax.rem(s, 2)
    second_to = 3 * lax.rem(s, 2)
    slot_there = lax.div(s, 2)

    loads = []

    def load(src, dst):
        single = pltpu.make_async_copy(src, dst, load_sems.at[len(loads)])
        single.start()
        loads.append(single)
        return single

    load_tokens = [load(ff_in, ff_own), load(cot_in, cot_own), load(near_in, cot_near)]
    load_weights = [load(w_gate, big.at[0]), load(w_up, big.at[1]), load(w_down, big.at[2])]
    load_after = load(after_in, after_attn)

    links.greet([links.core, links.xdev, links.ydev, links.z(1), links.z(2), links.z(3)])
    load_tokens[0].wait()
    near_x = links.send(ff_own.at[t], ff_near.at[t], links.xdev)

    def turned(source, place, target, first):
        flipped = source[place].T
        for part in range(2):
            for k in range(2):
                start = (2 * k + part) * block_rows

                def put(start=start, k=k):
                    target[k, :, first : first + pos] = flipped[start : start + block_rows]

                pl.when(x == part)(put)

    for place in range(2):
        turned(ff_own, place, ff_t, place * pos)
    for single in load_tokens[1:]:
        single.wait()
    for place in range(2):
        turned(cot_own, place, cot_t, place * pos)
        turned(cot_near, place, cot_t, (2 + place) * pos)
    for single in load_weights:
        single.wait()

    tile = 256

    def feed_forward(normed, cot, first):
        def step(index, carry):
            lanes = pl.ds(pl.multiple_of(index * tile, tile), tile)
            left = normed[...].reshape(2 * pos, width)
            gate = dot_f32(left, big[0, :, lanes])
            up = dot_f32(left, big[1, :, lanes])
            back = dot_f32(cot[...].reshape(2 * pos, width), big[2, :, lanes])
            for strip in range(0, 2 * pos, 64):
                part = slice(strip, strip + 64)
                square = gate[part] * gate[part]
                tanh = jnp.tanh(gelu_scale * gate[part] * (1.0 + 0.044715 * square))
                share = 0.5 * (1.0 + tanh)
                gelu = gate[part] * share
                slope = share + 0.5 * gate[part] * (1.0 - tanh * tanh) * (
                    gelu_scale * (1.0 + 3.0 * 0.044715 * square)
                )
                row = first + strip
                acts[row : row + 64, lanes] = (gelu * up[part]).astype(bf16)
                acts[1024 + row : 1088 + row, lanes] = (back[part] * up[part] * slope).astype(bf16)
                acts[2048 + row : 2112 + row, lanes] = (back[part] * gelu).astype(bf16)
            return carry

        lax.fori_loop(0, hidden // tile, step, 0)

    feed_forward(ff_own, cot_own, 0)

    def other_first(make, own_ref, send_slot, recv_slot):
        for start in range(0, width, tile):
            lanes = slice(start, min(start + tile, width))
            both = make(lanes)
            core_send[send_slot, :, lanes] = jnp.where(t == 0, both[pos:], both[:pos]).astype(bf16)
            own_ref[:, lanes] = jnp.where(t == 0, both[:pos], both[pos:])
        return links.send(core_send.at[send_slot], core_recv.at[recv_slot], links.core)

    back_core = other_first(
        lambda lanes: dot_f32(acts[1024 : 1024 + 2 * pos], big[0, lanes, :], NT)
        + dot_f32(acts[2048 : 2048 + 2 * pos], big[1, lanes, :], NT),
        mid,
        0,
        0,
    )
    branch_core = other_first(
        lambda lanes: dot_f32(acts[0 : 2 * pos], big[2, lanes, :], NT), spare, 1, 1
    )

    near_x.wait_recv()
    near_core = links.send(ff_near.at[t], ff_near.at[t], links.core)
    near_core.wait_recv()
    for place in range(2):
        turned(ff_near, place, ff_t, (2 + place) * pos)
    feed_forward(ff_near, cot_near, 2 * pos)

    lefts = (ff_t, ff_t, cot_t)
    sources = (1024, 2048, 0)
    order = (2, 0, 1)

    def grad_block(which, k, first):
        def step(index, carry):
            lanes = pl.ds(pl.multiple_of(index * tile, tile), tile)
            right = acts[sources[which] : sources[which] + 4 * pos, lanes]
            big[which, first : first + block_rows, lanes] = dot_f32(
                lefts[which][k], right
            ).astype(bf16)
            return carry

        lax.fori_loop(0, hidden // tile, step, 0)

    y_copies = {}
    for which in order:
        grad_block(which, 1 - y, 0)
        for start, size in row_parts:
            rows = slice(start, start + size)
            y_copies[which, start] = links.send(
                big.at[which, rows, :], y_recv.at[which, rows, :], links.ydev
            )
    for which in order:
        grad_block(which, y, block_rows)

    chunks = [(which, start, size) for which in order for start, size in row_parts]
    za_copies, zb_slots, stage_copies = {}, {}, [None, None]

    def serve_y(index):
        which, start, size = chunks[index]
        y_copies[which, start].wait_recv()
        own = slice(block_rows + start, block_rows + start + size)
        out = slice(2 * block_rows + start, 2 * block_rows + start + size)
        for part in range(2):
            lanes = slice(part * half, (part + 1) * half)
            total = big[which, own, lanes].astype(f32) + y_recv[
                which, start : start + size, lanes
            ].astype(f32)
            total = total.astype(bf16)

            def keep(total=total, lanes=lanes):
                big[which, own, 0:half] = total

            def give(total=total):
                big[which, out, 0:half] = total

            pl.when(keep_half == part)(keep)
            pl.when(send_half == part)(give)
        za_copies[index] = links.send(
            big.at[which, out, 0:half],
            za_recv.at[which, start : start + size, :],
            links.to_seq(pair_mate),
        )

    def zb_start(index, source, target, own):
        base = links.slots(3)
        zb_slots[index] = base
        one = links.copy(source(send_half), target(0), links.to_seq(first_to), base)
        two = links.copy(source(send_half), target(1), links.to_seq(first_to), base + 2)
        end = links.copy(source(keep_half), target(0), links.to_seq(second_to), base + 1)
        pl.when(slot_there == 0)(lambda: one.start())
        pl.when(slot_there == 1)(lambda: two.start())
        pl.when(inside)(lambda: end.start())
        pl.when(jnp.logical_not(inside))(own)

    def zb_wait(index, source, target):
        base = zb_slots[index]
        one = links.copy(source(send_half), target(0), links.to_seq(first_to), base)
        two = links.copy(source(send_half), target(1), links.to_seq(first_to), base + 2)
        end = links.copy(source(keep_half), target(0), links.to_seq(second_to), base + 1)

        def middle():
            one.wait_recv()
            two.wait_recv()

        pl.when(inside)(middle)
        pl.when(jnp.logical_not(inside))(lambda: end.wait_recv())

    def zb_sent(index, source, target):
        base = zb_slots[index]
        one = links.copy(source(send_half), target(0), links.to_seq(first_to), base)
        two = links.copy(source(send_half), target(1), links.to_seq(first_to), base + 2)
        end = links.copy(source(keep_half), target(0), links.to_seq(second_to), base + 1)
        pl.when(slot_there == 0)(lambda: one.wait_send())
        pl.when(slot_there == 1)(lambda: two.wait_send())
        pl.when(inside)(lambda: end.wait_send())

    def big_views(index):
        which, start, size = chunks[index]

        def source(part):
            first = 2 * block_rows + start
            return big.at[which, pl.ds(first + part * block_rows, size), half : half + 512]

        def target(place):
            return zb_recv.at[which, place, start : start + size, :]

        return source, target

    def serve_za(index):
        which, start, size = chunks[index]
        za_copies[index].wait_recv()
        total = big[which, block_rows + start : block_rows + start + size, 0:half].astype(
            f32
        ) + za_recv[which, start : start + size, :].astype(f32)
        total = total.astype(bf16)
        first = 2 * block_rows + start
        big[which, first : first + size, half : half + quarter] = total[:, :quarter]
        big[which, first + block_rows : first + block_rows + size, half : half + quarter] = total[
            :, quarter:
        ]
        source, target = big_views(index)

        def own():
            kept = jnp.where(keep_half == 0, total[:, :quarter], total[:, quarter:])
            zb_recv[which, 1, start : start + size, 0:quarter] = kept

        zb_start(index, source, target, own)

    def serve_zb(index):
        which, start, size = chunks[index]
        source, target = big_views(index)
        zb_wait(index, source, target)
        place = index % 2
        if stage_copies[place] is not None:
            stage_copies[place].wait()
        both = zb_recv[which, :, start : start + size, 0:quarter].astype(f32)
        stage[place, 0:size, :] = both[0] + both[1]
        stage_copies[place] = pltpu.make_async_copy(
            stage.at[place, 0:size, :],
            out_big.at[which, start : start + size, :],
            out_sems.at[place],
        )
        stage_copies[place].start()

    services = []
    for index in range(len(chunks) + 2):
        if index < len(chunks):
            services.append((serve_y, index))
        if 0 <= index - 1 < len(chunks):
            services.append((serve_za, index - 1))
        if 0 <= index - 2 < len(chunks):
            services.append((serve_zb, index - 2))
    services.reverse()

    def serve(amount):
        for _ in range(amount):
            if services:
                job, index = services.pop()
                job(index)

    links.sent(near_core)
    links.sent(near_x)
    small = load(w_small, acts.at[0:width, 0 : 4 * inner])
    load_n1 = load(normed_pair, ff_own)
    load_tok = load(tokens, ff_near.at[0])
    load_bias = load(bias_in, acts.at[:, 6 * pos : 7 * pos])
    load_pairs = [
        load(
            pairs_in.at[block, row],
            acts.at[
                kv_first + block * pos : kv_first + (block + 1) * pos,
                row * 2 * inner : (row + 1) * 2 * inner,
            ],
        )
        for block in range(4)
        for row in range(2)
    ]

    load_after.wait()
    back_core.wait_recv()

    def norm_back(inputs, grads, arrived, gain, added, out, low=None):
        def strip(index, total):
            rows = pl.ds(pl.multiple_of(index * 32, 32), 32)
            values = inputs(rows)
            scale = unit_scale(values)
            grad = grads[rows, :] + arrived[rows, :].astype(f32)
            gained = grad * gain[...]
            mean = jnp.mean(gained * values, axis=-1, keepdims=True)
            result = added(rows) + scale * gained - values * (scale * scale * scale * mean)
            out[rows, :] = result
            if low is not None:
                low[rows, :] = result.astype(bf16)
            return total + jnp.sum(grad * values * scale, axis=0, keepdims=True)

        return lax.fori_loop(0, pos // 32, strip, jnp.zeros((1, width), f32))

    vec[0] = jnp.zeros_like(vec[0])
    vec[0, 1:2, 0:width] = norm_back(
        lambda rows: after_attn[rows, :],
        mid,
        core_recv.at[0],
        gain_ff,
        lambda rows: cot_own[t, rows, :].astype(f32),
        mid,
        cot_near.at[t],
    )
    branch_send = links.send(cot_near.at[t], core_recv.at[2], links.core)
    branch_core.wait_recv()
    spare[...] = after_attn[...] + (spare[...] + core_recv[1].astype(f32))
    out_layer = pltpu.make_async_copy(spare, layer_out, out_sems.at[2])
    out_layer.start()
    branch_send.wait_recv()
    cot_near[1 - t] = core_recv[2]
    small.wait()

    def small_view(k, d):
        return (slice((d % 2) * 768 + k * inner, (d % 2) * 768 + (k + 1) * inner), 768 + 384 * (d // 2))

    def small_grads(k, left_of, rights):
        for d in range(4):
            rows, first = small_view(k, d)
            total = None
            for place in range(2):
                part = dot_f32(
                    left_of(place), rights[place, :, d * block_rows : (d + 1) * block_rows], TN
                )
                total = part if total is None else total + part
            acts[rows.start : rows.start + total.shape[0], first : first + block_rows] = (
                total.astype(bf16)
            )

    def small_rows(k_first, k_count):
        return slice(k_first * inner, (k_first + k_count) * inner)

    def small_source(k_first, k_count, dy, part):
        first_row = small_view(k_first, 2 * dy)[0].start + part * 768
        first = small_view(k_first, 2 * dy)[1]
        return acts.at[
            pl.ds(pl.multiple_of(first_row, 16), k_count * inner), first : first + 2 * inner
        ]

    def small_x(k_first, k_count):
        rows = small_rows(k_first, k_count)
        return [
            links.send(
                small_source(k_first, k_count, dy, 1 - x), gx_recv.at[dy, rows, :], links.xdev
            )
            for dy in range(2)
        ]

    def small_y(k_first, k_count, copies):
        for single in copies:
            single.wait_recv()
        rows = small_rows(k_first, k_count)
        for dy in range(2):
            total = small_source(k_first, k_count, dy, x)[...].astype(f32)
            total = (total + gx_recv[dy, rows].astype(f32)).astype(bf16)

            def keep(total=total):
                g_keep[k_first : k_first + k_count] = total.reshape(k_count, inner, 2 * inner)

            def give(total=total):
                gy_send[rows] = total

            pl.when(y == dy)(keep)
            pl.when(y != dy)(give)
        return links.send(gy_send.at[rows], gy_recv.at[rows], links.ydev)

    def small_za(k_first, k_count, single):
        single.wait_recv()
        ks = slice(k_first, k_first + k_count)
        other = gy_recv[small_rows(k_first, k_count)].reshape(k_count, inner, 2 * inner)
        g_keep[ks] = (g_keep[ks].astype(f32) + other.astype(f32)).astype(bf16)
        source = g_keep.at[ks, pl.ds(pl.multiple_of(send_half * 96, 16), 96), :]
        return links.send(source, gza_recv.at[ks], links.to_seq(pair_mate))

    def small_views(k_first, k_count):
        ks = slice(k_first, k_first + k_count)
        return (lambda part: gzb_send.at[part, ks]), (lambda place: gzb_recv.at[place, ks])

    def small_zb(k_first, k_count, single):
        single.wait_recv()
        ks = slice(k_first, k_first + k_count)
        kept = g_keep[ks, pl.ds(pl.multiple_of(keep_half * 96, 16), 96), :]
        total = (kept.astype(f32) + gza_recv[ks].astype(f32)).astype(bf16)
        gzb_send[0, ks] = total[:, :48]
        gzb_send[1, ks] = total[:, 48:]
        source, target = small_views(k_first, k_count)

        def own():
            gzb_recv[1, ks] = jnp.where(keep_half == 0, total[:, :48], total[:, 48:])

        zb_start(("small", k_first), source, target, own)

    def small_done(k_first, k_count):
        source, target = small_views(k_first, k_count)
        zb_wait(("small", k_first), source, target)
        for k in range(k_first, k_first + k_count):
            total = gzb_recv[0, k].astype(f32) + gzb_recv[1, k].astype(f32)
            out_small[k] = total.T[0:block_rows]

    for place in range(2):
        grad_ctx[place] = dot_f32(
            cot_near[place], acts[0:width, 3 * inner : 4 * inner]
        ).astype(bf16)
    small_grads(3, lambda place: context[place].astype(bf16), cot_near)
    out_x = small_x(3, 1)
    serve(1)

    anti = (
        lax.broadcasted_iota(jnp.int32, (pos, pos), 0)
        + lax.broadcasted_iota(jnp.int32, (pos, pos), 1)
        == pos - 1
    ).astype(bf16)

    def kv_place(row):
        return slice(768 + 2 * inner * row, 768 + 2 * inner * (row + 1))

    kv_za = []
    load_bias.wait()
    for single in load_pairs:
        single.wait()

    def kv_in(block, row, first):
        return acts[
            kv_first + block * pos : kv_first + (block + 1) * pos,
            row * 2 * inner + first : row * 2 * inner + first + dh,
        ]

    def bias_of(head, block):
        start = (head * 4 + block) * pos
        return acts[start : start + pos, 6 * pos : 7 * pos].astype(f32)

    for row in range(2):
        seg_query = seg_rows[row, :, pl.ds(pl.multiple_of(s * pos, 128), pos)]
        queries_t = []
        mixed = (grad_ctx[row].astype(f32) * context[row]).T
        for head in range(heads):
            lanes = slice(head * dh, (head + 1) * dh)
            query = queries[row, :, lanes]
            grad_head = grad_ctx[row, :, lanes]
            base = log_total[row, head : head + 1]
            delta = jnp.sum(mixed[head * dh : (head + 1) * dh], axis=0, keepdims=True)
            grad_qt = jnp.zeros((dh, pos), f32)
            for block in range(4):
                seg_key = seg_rows[row, :, block * pos : (block + 1) * pos]
                same = jnp.broadcast_to(seg_key, (pos, pos)).T == seg_query
                score = dot_f32(kv_in(block, row, head * dh), query, NT)
                score = score + bias_of(head, block)
                prob = jnp.exp(jnp.where(same, score, masked_score) - base)
                grad = dot_f32(kv_in(block, row, inner + head * dh), grad_head, NT)
                grad_score = (prob * (grad - delta)).astype(bf16)
                rows = slice(kv_first + block * pos, kv_first + (block + 1) * pos)
                first = kv_place(row).start
                acts[rows, first + head * dh : first + (head + 1) * dh] = dot_f32(
                    grad_score, query
                ).astype(bf16)
                acts[rows, first + inner + head * dh : first + inner + (head + 1) * dh] = dot_f32(
                    prob.astype(bf16), grad_head
                ).astype(bf16)
                grad_qt = grad_qt + dot_f32(kv_in(block, row, head * dh), grad_score, TN)
                sheared = jnp.concatenate(
                    [dot_f32(anti, grad_score), jnp.zeros((pos, pos), f32)], axis=1
                )
                sheared = pltpu.roll(sheared, 0, 1, stride=1, stride_axis=0)
                sums = jnp.sum(sheared, axis=0, keepdims=True)
                if row == 0:
                    diag[head, block : block + 1] = sums
                else:
                    diag[head, block : block + 1] = diag[head, block : block + 1] + sums
            queries_t.append(grad_qt)
            serve(1)
        grad_q[row] = jnp.concatenate(queries_t, axis=0).T.astype(bf16)
        source = acts.at[
            pl.ds(pl.multiple_of(kv_first + send_half * 2 * pos, 16), 2 * pos), kv_place(row)
        ]
        kv_za.append(links.send(source, kv_za_recv.at[row], links.to_seq(pair_mate)))
        if row == 0:
            out_y = small_y(3, 1, out_x)
    out_za = small_za(3, 1, out_y)

    window_ids = bucket_window[:, pl.ds(pl.multiple_of(s * pos, 128), 5 * pos)]
    table_ids = lax.broadcasted_iota(jnp.int32, (32, 5 * pos), 0)
    hot = (table_ids == window_ids).astype(f32)

    def put_entry(head, entry):
        vec[0, 2 + head : 3 + head, 0:32] = entry

    for head in range(heads):
        pieces = [jnp.zeros((1, pos), f32) for _ in range(5)]
        for block in range(4):
            pieces[3 - block] = pieces[3 - block] + diag[head, block : block + 1, 0:pos]
            pieces[4 - block] = pieces[4 - block] + diag[head, block : block + 1, pos : 2 * pos]
        line = jnp.concatenate(pieces, axis=1)
        entry = jnp.sum(hot * line, axis=1, keepdims=True)
        entry = jnp.broadcast_to(entry, (32, 128)).T[0:1]
        for core in range(2):
            pl.when(t == core)(
                lambda core=core, head=head, entry=entry: put_entry(core * heads + head, entry)
            )

    def kv_views(row):
        return (
            lambda part: ff_t.at[
                row, 0:pos, pl.ds(pl.multiple_of(part * 2 * inner, 128), 2 * inner)
            ],
            lambda place: kv_zb_recv.at[row, place],
        )

    for row in range(2):
        kv_za[row].wait_recv()
        kept = acts[
            pl.ds(pl.multiple_of(kv_first + keep_half * 2 * pos, 16), 2 * pos), kv_place(row)
        ]
        total = (kept.astype(f32) + kv_za_recv[row].astype(f32)).astype(bf16)
        ff_t[row, 0:pos, 0 : 2 * inner] = total[:pos]
        ff_t[row, 0:pos, 2 * inner : 4 * inner] = total[pos:]
        source, target = kv_views(row)

        def own(total=total, row=row):
            kv_zb_recv[row, 1] = jnp.where(keep_half == 0, total[:pos], total[pos:])

        zb_start(("kv", row), source, target, own)
    small_zb(3, 1, out_za)
    serve(2)
    out_layer.wait()
    grads_all = []
    for row in range(2):
        source, target = kv_views(row)
        zb_wait(("kv", row), source, target)
        both = (kv_zb_recv[row, 0].astype(f32) + kv_zb_recv[row, 1].astype(f32)).astype(bf16)
        grads_all.append(jnp.concatenate([grad_q[row], both], axis=1))
    load_n1.wait()
    qkv = slice(0, 3 * inner)
    for row in range(2):
        acts[2560 + row * pos : 2560 + (row + 1) * pos, qkv] = grads_all[row]
    links.sent(back_core)
    attn_core = other_first(
        lambda lanes: dot_f32(acts[2560 : 2560 + 2 * pos, qkv], acts[lanes, qkv], NT), spare, 0, 0
    )
    small_grads(0, lambda place: acts[2560 + place * pos : 2560 + (place + 1) * pos, qkv], ff_own)
    qkv_x = small_x(0, 3)
    attn_core.wait_recv()
    load_tok.wait()
    vec[0, 0:1, 0:width] = norm_back(
        lambda rows: ff_near[0, rows, :].astype(f32),
        spare,
        core_recv.at[0],
        gain_attn,
        lambda rows: mid[rows, :],
        spare,
    )
    vec_steps = [links.core, links.xdev, links.ydev, links.to_seq(pair_mate), links.z(2)]
    vec_copies = [links.send(vec.at[0], vec_recv.at[0], vec_steps[0])]

    def vec_next():
        step = len(vec_copies)
        vec_copies[-1].wait_recv()
        vec[step] = vec[step - 1] + vec_recv[step - 1]
        if step < 5:
            vec_copies.append(links.send(vec.at[step], vec_recv.at[step], vec_steps[step]))

    out_tokens = pltpu.make_async_copy(spare, grad_tokens, out_sems.at[3])
    out_tokens.start()
    serve(1)
    vec_next()
    qkv_y = small_y(0, 3, qkv_x)
    vec_next()
    serve(3)
    qkv_za = small_za(0, 3, qkv_y)
    vec_next()
    serve(3)
    small_zb(0, 3, qkv_za)
    vec_next()
    small_done(3, 1)
    serve(3)
    vec_next()
    out_vec[...] = vec[5]
    small_done(0, 3)
    serve(len(services))

    out_tokens.wait()
    for single in stage_copies:
        single.wait()
    for index in range(len(chunks)):
        zb_sent(index, *big_views(index))
    for row in range(2):
        zb_sent(("kv", row), *kv_views(row))
    zb_sent(("small", 3), *small_views(3, 1))
    zb_sent(("small", 0), *small_views(0, 3))
    links.finish()


def backward_part(weights, small, tokens, forward, seg_rows, bucket_window, gain_attn, gain_ff):
    w_gate, w_up, w_down = weights
    normed_pair, queries, pairs, context, log_total, after, ff_pair, cot_pair, cot_near, bias = forward
    pos, width = tokens.shape
    hidden = w_gate.shape[1]
    inner = queries.shape[2]
    shape = jax.ShapeDtypeStruct
    anywhere = pl.BlockSpec(memory_space=pl.ANY)
    rows = width // 4
    outs = (
        shape((pos, width), f32),
        shape((pos, width), f32),
        shape((3, rows, hidden // 4), f32),
        shape((4, rows, inner // 4), f32),
        shape((8, 1536), f32),
    )
    pair = pltpu.VMEM((2, pos, width), bf16)
    single = pltpu.VMEM((pos, width), f32)
    kv = pltpu.VMEM((2, 2, pos, 2 * inner), bf16)
    return pl.pallas_call(
        backward_kernel,
        out_shape=outs,
        in_specs=[anywhere] * 6
        + [vmem_spec(), anywhere]
        + [vmem_spec()] * 2
        + [anywhere] * 5
        + [vmem_spec()] * 4,
        out_specs=(anywhere, anywhere, anywhere, vmem_spec(), vmem_spec()),
        scratch_shapes=[
            pltpu.VMEM((3, width, hidden), bf16),
            pltpu.VMEM((3 * 4 * pos, hidden), bf16),
            pltpu.VMEM((2, rows, 4 * pos), bf16),
            pltpu.VMEM((2, rows, 4 * pos), bf16),
            pair,
            pair,
            pair,
            pair,
            single,
            single,
            single,
            pltpu.VMEM((3, rows, hidden), bf16),
            pltpu.VMEM((3, rows, hidden // 2), bf16),
            pltpu.VMEM((3, 2, rows, 512), bf16),
            pltpu.VMEM((2, 96, hidden // 4), f32),
            pltpu.VMEM((2, 2 * pos, 2 * inner), bf16),
            kv,
            pltpu.VMEM((2, 4 * inner, 2 * inner), bf16),
            pltpu.VMEM((4 * inner, 2 * inner), bf16),
            pltpu.VMEM((4, inner, 2 * inner), bf16),
            pltpu.VMEM((4 * inner, 2 * inner), bf16),
            pltpu.VMEM((4, inner // 2, 2 * inner), bf16),
            pltpu.VMEM((2, 4, inner // 4, 2 * inner), bf16),
            pltpu.VMEM((2, 4, inner // 4, 2 * inner), bf16),
            pltpu.VMEM((2, pos, width), bf16),
            pltpu.VMEM((3, pos, width), bf16),
            pltpu.VMEM((2, pos, inner), bf16),
            pltpu.VMEM((2, pos, inner), bf16),
            pltpu.VMEM((3, 4, 2 * pos), f32),
            pltpu.VMEM((6, 8, 1536), f32),
            pltpu.VMEM((5, 8, 1536), f32),
            pltpu.SemaphoreType.DMA((20,)),
            pltpu.SemaphoreType.DMA((4,)),
            pltpu.SemaphoreType.DMA((100,)),
            pltpu.SemaphoreType.DMA((100,)),
        ],
        compiler_params=pltpu.CompilerParams(
            collective_id=2, has_side_effects=True, vmem_limit_bytes=62 * 2**20
        ),
        name="backward_part",
    )(
        w_gate,
        w_up,
        w_down,
        small,
        normed_pair,
        tokens,
        queries,
        pairs,
        context,
        log_total,
        after,
        ff_pair,
        cot_pair,
        cot_near,
        bias,
        seg_rows,
        bucket_window,
        gain_attn,
        gain_ff,
    )


def shards_box(
    tokens,
    segment_ids,
    buckets,
    gain_attn,
    w_query,
    w_key,
    w_value,
    w_out,
    rel_table,
    gain_ff,
    w_gate,
    w_up,
    w_down,
    cotangent,
):
    seg_rows = segment_ids[:, None, :]
    bucket_window = jnp.pad(jnp.flip(buckets), (0, 1))[None]
    table_t = jnp.pad(rel_table.T, ((0, 5), (0, 0)))
    gain_rows = [gain.astype(jnp.float32)[None] for gain in (gain_attn, gain_ff)]
    forward = forward_part(
        tokens[0],
        cotangent[0],
        seg_rows,
        bucket_window,
        table_t,
        *gain_rows,
        w_query,
        w_key,
        w_value,
        w_out,
    )
    small = jnp.concatenate([w_query, w_key, w_value, w_out], axis=1)
    layer_out, grad_tokens, big, little, sums = backward_part(
        (w_gate, w_up, w_down), small, tokens[0], forward, seg_rows, bucket_window, *gain_rows
    )
    width = tokens.shape[2]
    return (
        layer_out[None],
        grad_tokens[None],
        sums[0, :width],
        little[0],
        little[1],
        little[2],
        little[3],
        sums[2:8, :32].T,
        sums[1, :width],
        big[0],
        big[1],
        big[2],
    )


def solution(mesh):
    sizes = tuple(mesh.shape[axis] for axis in ("dp", "tensor", "seq"))
    part = shards_box if sizes == (4, 2, 4) else shards
    return jax.shard_map(
        part,
        mesh=mesh,
        in_specs=(
            P(("dp", "tensor"), "seq", None),
            P("dp", None),
            P(),
            P(),
            P(None, "tensor"),
            P(None, "tensor"),
            P(None, "tensor"),
            P(None, "tensor"),
            P(None, "tensor"),
            P(),
            P(None, "tensor"),
            P(None, "tensor"),
            P(None, "tensor"),
            P(("dp", "tensor"), "seq", None),
        ),
        out_specs=(
            P(("dp", "tensor"), "seq", None),
            P(("dp", "tensor"), "seq", None),
            P(),
            P("dp", ("tensor", "seq")),
            P("dp", ("tensor", "seq")),
            P("dp", ("tensor", "seq")),
            P("dp", ("tensor", "seq")),
            P(),
            P(),
            P("dp", ("tensor", "seq")),
            P("dp", ("tensor", "seq")),
            P("dp", ("tensor", "seq")),
        ),
        check_vma=False,
    )
```
